256 devices in a mesh: row: 16 (over x_hi, z), col: 16 (over y, x_lo, core).
Axes of the slice: x: 4 (x_hi: 2, x_lo: 2; x = x_hi * 2 + x_lo), y: 4, z: 8, core: 2. Of those that a mesh axis runs over, the one named last changes fastest.
Arguments:
- streamwise: float32 [384, 256, 1024], P('row', 'col'), may hold values from -6 to 6
- wallnormal: float32 [384, 256, 1024], P('row', 'col'), may hold values from -6 to 6
- spanwise: float32 [384, 256, 1024], P('row', 'col'), may hold values from -6 to 6
- deriv_x: bfloat16 [2, 1024, 1024], replicated, may hold values from -0.1875 to 0.1875
- deriv_y: bfloat16 [2, 384, 384], replicated, may hold values from -0.3125 to 0.3125
- deriv_z: bfloat16 [2, 256, 256], replicated, may hold values from -0.375 to 0.375
Outputs:
- momentum_term: float32 [384, 256, 1024], P('row', 'col')
The draws below stay inside these ranges and needn't reach their ends.
All inputs are finite; a program needn't handle non-finite values.
Results may differ from the reference program's by a relative error of at most 0.0003.
Values sent between devices are 32-bit elements; how exact they have to be, the bound alone decides.
A program may use at most 128 MiB of HBM per device.

```python
import jax
import jax.numpy as jnp
from jax import lax

NX = 1024
NY = 384
NZ = 256


def block_levels(rng, dims, cuts, smallest, top_value):
    def one(dim, shards_of):
        heights = jax.random.uniform(jax.random.fold_in(jax.random.fold_in(rng, 6), dim), (shards_of,), jnp.float32, smallest / len(cuts), top_value / len(cuts))
        return jnp.repeat(jnp.exp(heights), dims[dim] // shards_of).reshape((-1,) + (1,) * (len(dims) - dim - 1))

    factor_of = one(*cuts[0])
    for cut in cuts[1:]:
        factor_of = factor_of * one(*cut)
    return factor_of


def gaussian(rng, shape, deviation, reach, split=(), held_as=jnp.bfloat16):
    array = deviation * jax.random.normal(rng, shape, jnp.float32)
    if split:
        array = array * block_levels(rng, shape, split, -0.22, 0.18)
    return jnp.clip(array, -reach, reach).astype(held_as)


def setup_inputs(seed: int = 0) -> dict:
    key_list = jax.random.split(jax.random.key(seed), 7)
    streamwise = gaussian(key_list[0], (NY, NZ, NX), 1.0, 6.0, ((0, 16), (1, 16)), jnp.float32)
    wallnormal = gaussian(key_list[1], (NY, NZ, NX), 1.0, 6.0, ((0, 16), (1, 16)), jnp.float32)
    spanwise = gaussian(key_list[2], (NY, NZ, NX), 1.0, 6.0, ((0, 16), (1, 16)), jnp.float32)
    deriv_x = gaussian(key_list[3], (2, NX, NX), NX ** -0.5, 0.1875)
    deriv_y = gaussian(key_list[4], (2, NY, NY), NY ** -0.5, 0.3125)
    deriv_z = gaussian(key_list[5], (2, NZ, NZ), NZ ** -0.5, 0.375)
    return {"streamwise": streamwise, "wallnormal": wallnormal, "spanwise": spanwise, "deriv_x": deriv_x, "deriv_y": deriv_y, "deriv_z": deriv_z}


viscosity = 0.5


def reference(streamwise, wallnormal, spanwise, deriv_x, deriv_y, deriv_z):
    high = lax.Precision.HIGHEST
    mat_x = deriv_x.astype(jnp.float32)
    mat_y = deriv_y.astype(jnp.float32)
    mat_z = deriv_z.astype(jnp.float32)
    first = jnp.einsum('azj,ij->azi', streamwise, mat_x[0], precision=high)
    second = jnp.einsum('azj,ij->azi', streamwise, mat_x[1], precision=high)
    total = -streamwise * first + viscosity * second
    first = jnp.einsum('ij,jzx->izx', mat_y[0], streamwise, precision=high)
    second = jnp.einsum('ij,jzx->izx', mat_y[1], streamwise, precision=high)
    total = total - wallnormal * first + viscosity * second
    first = jnp.einsum('ij,ajx->aix', mat_z[0], streamwise, precision=high)
    second = jnp.einsum('ij,ajx->aix', mat_z[1], streamwise, precision=high)
    total = total - spanwise * first + viscosity * second
    return total
```

```python
import functools

import jax
import jax.numpy as jnp
from jax import lax
from jax.experimental import pallas as pl
from jax.experimental.pallas import tpu as pltpu
from jax.sharding import PartitionSpec as P

viscosity = 0.5
MESH = pl.DeviceIdType.MESH
CUTS = 2
ROWS_OF_CUT = 8 // CUTS


def split(value):
    high = value.astype(jnp.bfloat16)
    low = (value - high.astype(jnp.float32)).astype(jnp.bfloat16)
    return high, low


def product(matrix, value):
    high, low = split(value)
    return jnp.dot(matrix, high, preferred_element_type=jnp.float32) + jnp.dot(
        matrix, low, preferred_element_type=jnp.float32
    )


def kernel(
    u_hbm, v_hbm, w_hbm, mx_hbm, my_hbm, mz_hbm, out_hbm,
    u_own, v_own, u_high, mat_x, mat_y, mat_z, u_stage, v_stage,
    u_y, v_y, term_y, back_y, u_z, w_z, term_z, back_z, total,
    load_sem, send_sem, row_sem, col_sem,
):
    row = lax.axis_index("row")
    col = lax.axis_index("col")
    x_low = (col // 2) % 2
    mine = (col // 4) * 2 + col % 2

    def row_peer(shift):
        return lax.rem(row + shift, 16)

    def col_peer(shift):
        other = lax.rem(mine + shift, 8)
        return other, (other // 2) * 4 + x_low * 2 + other % 2

    partner = col + 2 - 4 * x_low

    def lanes_of(x):
        return slice(x * 128, (x + 1) * 128)

    for x in range(8):
        pltpu.make_async_copy(u_hbm.at[:, :, lanes_of(x)], u_own.at[x], load_sem.at[0]).start()
    for x in range(8):
        pltpu.make_async_copy(v_hbm.at[:, :, lanes_of(x)], v_own.at[x], load_sem.at[1]).start()

    barrier = pltpu.get_barrier_semaphore()

    @pl.loop(1, 16)
    def _(shift):
        pl.semaphore_signal(barrier, inc=1, device_id=(row_peer(shift), col), device_id_type=MESH)

    @pl.loop(1, 8)
    def _(shift):
        pl.semaphore_signal(
            barrier, inc=1, device_id=(row, col_peer(shift)[1]), device_id_type=MESH
        )

    pl.semaphore_signal(barrier, inc=1, device_id=(row, partner), device_id_type=MESH)
    pltpu.make_async_copy(mx_hbm, mat_x, load_sem.at[2]).start()
    pltpu.make_async_copy(my_hbm, mat_y, load_sem.at[3]).start()
    pltpu.make_async_copy(mz_hbm, mat_z, load_sem.at[4]).start()

    def restage(own, stage):
        flat = own.reshape(8 * 24 * 16, 128)

        @pl.loop(0, 16)
        def _(z):
            for x in range(8):
                stage[x, z] = flat[pl.ds(x * 384 + z, 24, stride=16), :]

    def send_row(stage, pencil, kind):
        for cut in range(CUTS):
            rows = pl.ds(cut * ROWS_OF_CUT, ROWS_OF_CUT)

            def piece(to):
                return (
                    stage.at[
                        lax.rem(to, 8),
                        pl.ds((to // 8) * 8 + cut * ROWS_OF_CUT, ROWS_OF_CUT),
                    ],
                    pencil.at[rows, pl.ds(pl.multiple_of(row * 24, 8), 24), :],
                )

            def send(shift):
                to = row_peer(shift)
                src, dst = piece(to)
                pltpu.make_async_remote_copy(
                    src_ref=src, dst_ref=dst, send_sem=send_sem.at[kind],
                    recv_sem=row_sem.at[kind, cut], device_id=(to, col), device_id_type=MESH,
                ).start()

            @pl.loop(1, 8)
            def _(shift):
                send(shift)
                send(16 - shift)

            send(8)
            src, dst = piece(row)
            pltpu.make_async_copy(src, dst, row_sem.at[kind, cut]).start()

    def send_col(field, pencil, kind):
        for cut in range(3):

            def piece(to):
                if kind == 0:
                    dst = pencil.at[
                        cut, col // 4, pl.ds(pl.multiple_of((col % 4) * 16, 16), 16), :
                    ]
                else:
                    dst = pencil.at[cut, pl.ds(pl.multiple_of(mine * 16, 16), 16), :]
                return field.at[to * 3 + cut], dst

            @pl.loop(1, 8)
            def _(shift):
                to, to_col = col_peer(shift)
                src, dst = piece(to)
                pltpu.make_async_remote_copy(
                    src_ref=src, dst_ref=dst, send_sem=send_sem.at[3 + kind],
                    recv_sem=col_sem.at[kind, cut], device_id=(row, to_col), device_id_type=MESH,
                ).start()

            src, dst = piece(mine)
            pltpu.make_async_copy(src, dst, col_sem.at[kind, cut]).start()

    def arrived(ref, sem):
        pltpu.make_async_copy(ref, ref, sem).wait()

    arrived(u_own, load_sem.at[0])
    restage(u_own, u_stage)
    pl.semaphore_wait(barrier, 23)
    send_row(u_stage, u_y, 0)
    send_col(u_hbm, u_z, 0)
    arrived(v_own, load_sem.at[1])
    restage(v_own, v_stage)
    send_row(v_stage, v_y, 1)
    send_col(w_hbm, w_z, 1)

    flat_total = total.reshape(8 * 24 * 16, 128)

    for x in range(8):
        high, low = split(u_own[x].reshape(384, 128))
        u_high[:384, lanes_of(x)] = high
        u_high[384:, lanes_of(x)] = low

    arrived(mat_x, load_sem.at[2])

    @pl.loop(0, 4)
    def _(part):
        at = pl.multiple_of(part * 256, 256)

        def along(which):
            both = lax.dot_general(
                u_high[...], mat_x[which, pl.ds(at, 256), :],
                (((1,), (1,)), ((), ())), preferred_element_type=jnp.float32,
            )
            return both[:384] + both[384:]

        first, second = along(0), along(1)
        for i in range(2):
            here = u_own[part * 2 + i].reshape(384, 128)
            term = -here * first[:, lanes_of(i)] + viscosity * second[:, lanes_of(i)]
            total[part * 2 + i] = term.reshape(24, 16, 128)

    arrived(mat_y, load_sem.at[3])
    arrived(mat_z, load_sem.at[4])

    half = pl.ds(pl.multiple_of(x_low * 32, 32), 32)
    other_half = pl.ds(pl.multiple_of(32 - x_low * 32, 32), 32)

    def swap(cut):
        region = u_z.at[cut, :, half, :]
        return pltpu.make_async_remote_copy(
            src_ref=region, dst_ref=region, send_sem=send_sem.at[5],
            recv_sem=col_sem.at[3, cut], device_id=(row, partner), device_id_type=MESH,
        )

    def work_y(cut):
        arrived(u_y.at[pl.ds(cut * ROWS_OF_CUT, ROWS_OF_CUT)], row_sem.at[0, cut])
        arrived(v_y.at[pl.ds(cut * ROWS_OF_CUT, ROWS_OF_CUT)], row_sem.at[1, cut])
        matrix = mat_y[...].reshape(768, 384)

        @pl.loop(0, ROWS_OF_CUT // 2)
        def _(pair):
            z = cut * ROWS_OF_CUT + pair * 2
            both = product(matrix, jnp.concatenate([u_y[z], u_y[z + 1]], axis=1))
            for i in range(2):
                lanes = slice(i * 128, (i + 1) * 128)
                term_y[z + i] = -v_y[z + i] * both[:384, lanes] + viscosity * both[384:, lanes]

        rows = pl.ds(cut * ROWS_OF_CUT, ROWS_OF_CUT)

        def piece(to):
            return (
                term_y.at[rows, pl.ds(pl.multiple_of(to * 24, 8), 24), :],
                back_y.at[
                    lax.rem(row, 8), pl.ds((row // 8) * 8 + cut * ROWS_OF_CUT, ROWS_OF_CUT)
                ],
            )

        def send(shift):
            to = row_peer(shift)
            src, dst = piece(to)
            pltpu.make_async_remote_copy(
                src_ref=src, dst_ref=dst, send_sem=send_sem.at[2],
                recv_sem=row_sem.at[2, cut], device_id=(to, col), device_id_type=MESH,
            ).start()

        @pl.loop(1, 8)
        def _(shift):
            send(shift)
            send(16 - shift)

        send(8)
        src, dst = piece(row)
        pltpu.make_async_copy(src, dst, row_sem.at[2, cut]).start()

    def work_z(cut):
        arrived(u_z.at[cut, :, other_half, :], col_sem.at[3, cut])
        arrived(w_z.at[cut], col_sem.at[1, cut])
        matrix = mat_z[:, :, half, :].reshape(256, 256)
        for tile in range(4):
            lanes = slice(tile * 256, (tile + 1) * 256)
            both = product(matrix, u_z[cut, :, :, lanes].reshape(256, 256))
            term_z[cut, :, lanes] = (
                -w_z[cut, :, lanes] * both[:128] + viscosity * both[128:]
            )

        def piece(to):
            return (
                term_z.at[cut, pl.ds(pl.multiple_of(to * 16, 16), 16), :],
                back_z.at[mine * 3 + cut],
            )

        @pl.loop(1, 8)
        def _(shift):
            to, to_col = col_peer(shift)
            src, dst = piece(to)
            pltpu.make_async_remote_copy(
                src_ref=src, dst_ref=dst, send_sem=send_sem.at[6],
                recv_sem=col_sem.at[2, cut], device_id=(row, to_col), device_id_type=MESH,
            ).start()

        src, dst = piece(mine)
        pltpu.make_async_copy(src, dst, col_sem.at[2, cut]).start()

    for cut in range(3):
        arrived(u_z.at[cut, :, half, :], col_sem.at[0, cut])
        swap(cut).start()
    for cut in range(3):
        work_z(cut)
        if cut < CUTS:
            work_y(cut)
    for cut in range(3, CUTS):
        work_y(cut)

    for cut in range(3):
        arrived(back_z.at[pl.ds(cut * 8, 8)], col_sem.at[2, cut])

    @pl.loop(0, 24)
    def _(y):
        for x in range(8):
            total[x, y] += back_z[y, :, lanes_of(x)]

    for cut in range(CUTS):
        arrived(back_y.at[:, pl.ds(cut * 2 * ROWS_OF_CUT, 2 * ROWS_OF_CUT)], row_sem.at[2, cut])
        for upper in range(2):

            @pl.loop(0, ROWS_OF_CUT)
            def _(step):
                z = upper * 8 + cut * ROWS_OF_CUT + step
                for x in range(8):
                    flat_total[pl.ds(x * 384 + z, 24, stride=16), :] += back_y[x, z]

    for x in range(8):
        pltpu.make_async_copy(total.at[x], out_hbm.at[:, :, lanes_of(x)], load_sem.at[5]).start()

    arrived(u_stage.at[:, pl.ds(0, 15)], send_sem.at[0])
    arrived(v_stage.at[:, pl.ds(0, 15)], send_sem.at[1])
    arrived(back_y.at[:, pl.ds(0, 15)], send_sem.at[2])
    arrived(back_z.at[pl.ds(0, 21)], send_sem.at[3])
    arrived(back_z.at[pl.ds(0, 21)], send_sem.at[4])
    arrived(back_z, send_sem.at[5])
    arrived(back_z.at[pl.ds(0, 21)], send_sem.at[6])
    arrived(total, load_sem.at[5])


def shards(u, v, w, deriv_x, deriv_y, deriv_z):
    f32, bf16 = jnp.float32, jnp.bfloat16
    field = pltpu.VMEM((24, 16, 1024), f32)
    tiled = pltpu.VMEM((8, 24, 16, 128), f32)
    staged = pltpu.VMEM((8, 16, 24, 128), f32)
    pencil_y = pltpu.VMEM((8, 384, 128), f32)
    half_z = pltpu.VMEM((3, 128, 1024), f32)
    return pl.pallas_call(
        kernel,
        out_shape=jax.ShapeDtypeStruct((24, 16, 1024), f32),
        in_specs=[pl.BlockSpec(memory_space=pl.ANY)] * 6,
        out_specs=pl.BlockSpec(memory_space=pl.ANY),
        scratch_shapes=[
            tiled, tiled, pltpu.VMEM((768, 1024), bf16),
            pltpu.VMEM((2, 1024, 1024), bf16), pltpu.VMEM((2, 384, 384), bf16),
            pltpu.VMEM((2, 4, 64, 256), bf16),
            staged, staged, pencil_y, pencil_y, pencil_y, staged,
            pltpu.VMEM((3, 4, 64, 1024), f32), half_z, half_z, field, tiled,
            pltpu.SemaphoreType.DMA((6,)), pltpu.SemaphoreType.DMA((7,)),
            pltpu.SemaphoreType.DMA((3, CUTS)), pltpu.SemaphoreType.DMA((4, 3)),
        ],
        compiler_params=pltpu.CompilerParams(
            collective_id=0, has_side_effects=True, vmem_limit_bytes=52 * 2**20
        ),
        cost_estimate=pl.CostEstimate(flops=5 * 10**9, bytes_accessed=12 * 2**20, transcendentals=0),
        name="momentum",
    )(u, v, w, deriv_x, deriv_y, deriv_z.reshape(2, 4, 64, 256))


def solution(mesh):
    placed = (P("row", "col", None), P("row", "col", None), P("row", "col", None), P(), P(), P())
    return jax.shard_map(
        shards, mesh=mesh, in_specs=placed, out_specs=P("row", "col", None), check_vma=False
    )
```

```python
import functools

import jax
import jax.numpy as jnp
from jax import lax
from jax.experimental import pallas as pl
from jax.experimental.pallas import tpu as pltpu
from jax.sharding import PartitionSpec as P

viscosity = 0.5
MESH = pl.DeviceIdType.MESH
CUTS = 2
ROWS_OF_CUT = 8 // CUTS


def split(value):
    high = value.astype(jnp.bfloat16)
    low = (value - high.astype(jnp.float32)).astype(jnp.bfloat16)
    return high, low


def product(matrix, value):
    high, low = split(value)
    return jnp.dot(matrix, high, preferred_element_type=jnp.float32) + jnp.dot(
        matrix, low, preferred_element_type=jnp.float32
    )


def kernel(
    u_hbm, v_hbm, w_hbm, mx_hbm, my_hbm, mz_hbm, total,
    u_own, v_own, u_high, mat_x, mat_y, mat_z, rows_y, lhs_y, u_stage, v_stage,
    u_y, v_y, term_y, back_y, u_z, w_z, term_z, back_z,
    load_sem, send_sem, row_sem, col_sem,
):
    row = lax.axis_index("row")
    col = lax.axis_index("col")
    x_low = (col // 2) % 2
    mine = (col // 4) * 2 + col % 2

    x_me, z_me = row // 8, lax.rem(row, 8)

    def around(z):
        return lax.rem(z + 8, 8)

    def row_of(x, z):
        return x * 8 + around(z)

    def col_peer(shift):
        other = lax.rem(mine + shift, 8)
        return other, (other // 2) * 4 + x_low * 2 + other % 2

    partner = col + 2 - 4 * x_low

    def lanes_of(x):
        return slice(x * 128, (x + 1) * 128)

    for x in range(8):
        pltpu.make_async_copy(u_hbm.at[:, :, lanes_of(x)], u_own.at[x], load_sem.at[0]).start()
    for x in range(8):
        pltpu.make_async_copy(v_hbm.at[:, :, lanes_of(x)], v_own.at[x], load_sem.at[1]).start()

    barrier = pltpu.get_barrier_semaphore()

    def greet(x, z):
        pl.semaphore_signal(barrier, inc=1, device_id=(row_of(x, z), col), device_id_type=MESH)

    @pl.loop(1, 4)
    def _(j):
        for z in (z_me + j, z_me - j):
            greet(x_me, z)
            greet(1 - x_me, z)

    greet(1 - x_me, z_me)

    @pl.loop(1, 8)
    def _(shift):
        pl.semaphore_signal(
            barrier, inc=1, device_id=(row, col_peer(shift)[1]), device_id_type=MESH
        )

    pl.semaphore_signal(barrier, inc=1, device_id=(row, partner), device_id_type=MESH)
    pltpu.make_async_copy(mx_hbm, mat_x, load_sem.at[2]).start()
    pltpu.make_async_copy(my_hbm, mat_y, load_sem.at[3]).start()
    pltpu.make_async_copy(mz_hbm, mat_z, load_sem.at[4]).start()

    def restage(own, stage, cut):
        flat = own.reshape(8 * 24 * 16, 128)
        for upper in range(2):

            @pl.loop(0, ROWS_OF_CUT)
            def _(step):
                z = upper * 8 + cut * ROWS_OF_CUT + step
                for x in range(8):
                    stage[x, z] = flat[pl.ds(x * 384 + z, 24, stride=16), :]

    def over_row(piece, kind, cut, sems):
        def send(x, j, role):
            src, dst, to = piece(x, j, role)
            pltpu.make_async_remote_copy(
                src_ref=src, dst_ref=dst, send_sem=send_sem.at[kind],
                recv_sem=sems(role), device_id=(to, col), device_id_type=MESH,
            ).start()

        @pl.loop(0, 3)
        def _(step):
            for role in range(2):
                send(1 - x_me, 3 - step, role)
                send(x_me, 3 - step, role)

        for role in range(2):
            send(1 - x_me, 0, role)
            src, dst, _ = piece(x_me, 0, role)
            pltpu.make_async_copy(src, dst, sems(role)).start()

    def send_row(stage, pencil, kind, cut):
        rows = pl.ds(cut * ROWS_OF_CUT, ROWS_OF_CUT)

        def piece(x, j, role):
            to = around(z_me + j) if role == 0 else around(z_me - j)
            group = to if role == 0 else around(to - 1)
            src = stage.at[group, pl.ds(x * 8 + cut * ROWS_OF_CUT, ROWS_OF_CUT)]
            if kind == 0:
                dst = pencil.at[role, rows, x_me, pl.ds(pl.multiple_of(z_me * 24, 8), 24), :]
            else:
                slot = x_me * 4 + (3 - j if role == 0 else j)
                dst = pencil.at[role, rows, pl.ds(pl.multiple_of(slot * 24, 8), 24), :]
            return src, dst, x * 8 + to

        over_row(piece, kind, cut, lambda role: row_sem.at[kind * 2 + role, cut])

    def exchange(role, cut):
        to = row_of(x_me, z_me + 1 - 2 * role)

        @pl.loop(0, 4)
        def _(i):
            z = around(z_me - 3 + i + 3 * role)
            at = pl.ds(pl.multiple_of(z * 24, 8), 24)
            rows = pl.ds(cut * ROWS_OF_CUT, ROWS_OF_CUT)
            pltpu.make_async_remote_copy(
                src_ref=u_y.at[role, rows, :, at, :],
                dst_ref=u_y.at[1 - role, rows, :, at, :],
                send_sem=send_sem.at[7], recv_sem=row_sem.at[5 + 1 - role, cut],
                device_id=(to, col), device_id_type=MESH,
            ).start()

    def send_col(field, pencil, kind):
        for cut in range(3):

            def piece(to):
                if kind == 0:
                    dst = pencil.at[
                        cut, col // 4, pl.ds(pl.multiple_of((col % 4) * 16, 16), 16), :
                    ]
                else:
                    dst = pencil.at[cut, pl.ds(pl.multiple_of(mine * 16, 16), 16), :]
                return field.at[to * 3 + cut], dst

            @pl.loop(1, 8)
            def _(shift):
                to, to_col = col_peer(shift)
                src, dst = piece(to)
                pltpu.make_async_remote_copy(
                    src_ref=src, dst_ref=dst, send_sem=send_sem.at[3 + kind],
                    recv_sem=col_sem.at[kind, cut], device_id=(row, to_col), device_id_type=MESH,
                ).start()

            src, dst = piece(mine)
            pltpu.make_async_copy(src, dst, col_sem.at[kind, cut]).start()

    def arrived(ref, sem):
        pltpu.make_async_copy(ref, ref, sem).wait()

    arrived(u_own, load_sem.at[0])
    restage(u_own, u_stage, 0)
    pl.semaphore_wait(barrier, 21)
    send_row(u_stage, u_y, 0, 0)
    send_col(u_hbm, u_z, 0)
    for cut in range(1, CUTS):
        restage(u_own, u_stage, cut)
        send_row(u_stage, u_y, 0, cut)
    arrived(v_own, load_sem.at[1])
    for cut in range(CUTS):
        restage(v_own, v_stage, cut)
        send_row(v_stage, v_y, 1, cut)
    send_col(w_hbm, w_z, 1)

    flat_total = total.reshape(8 * 24 * 16, 128)

    for x in range(8):
        high, low = split(u_own[x].reshape(384, 128))
        u_high[:384, lanes_of(x)] = high
        u_high[384:, lanes_of(x)] = low

    arrived(mat_x, load_sem.at[2])

    @pl.loop(0, 4)
    def _(part):
        at = pl.multiple_of(part * 256, 256)

        def along(which):
            both = lax.dot_general(
                u_high[...], mat_x[which, pl.ds(at, 256), :],
                (((1,), (1,)), ((), ())), preferred_element_type=jnp.float32,
            )
            return both[:384] + both[384:]

        first, second = along(0), along(1)
        for i in range(2):
            here = u_own[part * 2 + i].reshape(384, 128)
            term = -here * first[:, lanes_of(i)] + viscosity * second[:, lanes_of(i)]
            total[part * 2 + i] = term.reshape(24, 16, 128)

    arrived(mat_y, load_sem.at[3])
    arrived(mat_z, load_sem.at[4])

    rows_y[...] = mat_y[...].astype(jnp.float32)
    for role in range(2):
        for which in range(2):
            for x in range(2):
                for pair in range(2):
                    some = []
                    for j in (2 * pair, 2 * pair + 1):
                        z = around(z_me - 3 + j + 3 * role)
                        at = pl.multiple_of(x * 192 + z * 24, 8)
                        some.append(rows_y[which, pl.ds(at, 24), :])
                    start = which * 192 + x * 96 + pair * 48
                    lhs_y[role, start : start + 48, :] = jnp.concatenate(some, axis=0).astype(
                        jnp.bfloat16
                    )

    half = pl.ds(pl.multiple_of(x_low * 32, 32), 32)
    other_half = pl.ds(pl.multiple_of(32 - x_low * 32, 32), 32)

    def swap(cut):
        region = u_z.at[cut, :, half, :]
        return pltpu.make_async_remote_copy(
            src_ref=region, dst_ref=region, send_sem=send_sem.at[5],
            recv_sem=col_sem.at[3, cut], device_id=(row, partner), device_id_type=MESH,
        )

    def own_half(role, cut):
        arrived(v_y.at[role, pl.ds(cut * ROWS_OF_CUT, ROWS_OF_CUT)], row_sem.at[role, cut])

    def work_y(role, cut):
        rows = pl.ds(cut * ROWS_OF_CUT, ROWS_OF_CUT)
        arrived(v_y.at[role, rows], row_sem.at[5 + role, cut])
        arrived(v_y.at[role, rows], row_sem.at[2 + role, cut])

        @pl.loop(0, ROWS_OF_CUT // 2)
        def _(pair):
            z = cut * ROWS_OF_CUT + pair * 2
            both = product(
                lhs_y[role],
                jnp.concatenate(
                    [u_y[role, z + i].reshape(384, 128) for i in range(2)], axis=1
                ),
            )
            for i in range(2):
                lanes = lanes_of(i)
                term_y[role, z + i] = (
                    -v_y[role, z + i] * both[:192, lanes] + viscosity * both[192:, lanes]
                )

    def return_y(cut):
        rows = pl.ds(cut * ROWS_OF_CUT, ROWS_OF_CUT)

        def piece(x, j, role):
            to = around(z_me - j) if role == 0 else around(z_me + j)
            slot = x * 4 + (3 - j if role == 0 else j)
            return (
                term_y.at[role, rows, pl.ds(pl.multiple_of(slot * 24, 8), 24), :],
                back_y.at[
                    around(z_me - role), pl.ds(x_me * 8 + cut * ROWS_OF_CUT, ROWS_OF_CUT)
                ],
                x * 8 + to,
            )

        over_row(piece, 2, cut, lambda role: row_sem.at[4, cut])

    def work_z(cut):
        arrived(u_z.at[cut, :, other_half, :], col_sem.at[3, cut])
        arrived(w_z.at[cut], col_sem.at[1, cut])
        matrix = mat_z[:, :, half, :].reshape(256, 256)
        for tile in range(4):
            lanes = slice(tile * 256, (tile + 1) * 256)
            both = product(matrix, u_z[cut, :, :, lanes].reshape(256, 256))
            term_z[cut, :, lanes] = (
                -w_z[cut, :, lanes] * both[:128] + viscosity * both[128:]
            )

        def piece(to):
            return (
                term_z.at[cut, pl.ds(pl.multiple_of(to * 16, 16), 16), :],
                back_z.at[mine * 3 + cut],
            )

        @pl.loop(1, 8)
        def _(shift):
            to, to_col = col_peer(shift)
            src, dst = piece(to)
            pltpu.make_async_remote_copy(
                src_ref=src, dst_ref=dst, send_sem=send_sem.at[6],
                recv_sem=col_sem.at[2, cut], device_id=(row, to_col), device_id_type=MESH,
            ).start()

        src, dst = piece(mine)
        pltpu.make_async_copy(src, dst, col_sem.at[2, cut]).start()

    for cut in range(3):
        arrived(u_z.at[cut, :, half, :], col_sem.at[0, cut])
        swap(cut).start()
    for cut in range(CUTS):
        for role in range(2):
            own_half(role, cut)
            exchange(role, cut)
    for cut in range(max(3, CUTS)):
        if cut < 3:
            work_z(cut)
        if cut < CUTS:
            work_y(0, cut)
            work_y(1, cut)
            return_y(cut)

    for cut in range(3):
        arrived(back_z.at[pl.ds(cut * 8, 8)], col_sem.at[2, cut])

    @pl.loop(0, 24)
    def _(y):
        for x in range(8):
            total[x, y] += back_z[y, :, lanes_of(x)]

    for cut in range(CUTS):
        arrived(back_y.at[:, pl.ds(cut * 2 * ROWS_OF_CUT, 2 * ROWS_OF_CUT)], row_sem.at[4, cut])
        for upper in range(2):

            @pl.loop(0, ROWS_OF_CUT)
            def _(step):
                z = upper * 8 + cut * ROWS_OF_CUT + step
                for x in range(8):
                    flat_total[pl.ds(x * 384 + z, 24, stride=16), :] += back_y[x, z]

    arrived(u_stage.at[:, pl.ds(0, 14)], send_sem.at[0])
    arrived(v_stage.at[:, pl.ds(0, 14)], send_sem.at[1])
    arrived(back_y.at[:, pl.ds(0, 14)], send_sem.at[2])
    arrived(back_y, send_sem.at[7])
    arrived(back_z.at[pl.ds(0, 21)], send_sem.at[3])
    arrived(back_z.at[pl.ds(0, 21)], send_sem.at[4])
    arrived(back_z, send_sem.at[5])
    arrived(back_z.at[pl.ds(0, 21)], send_sem.at[6])


def shards(u, v, w, deriv_x, deriv_y, deriv_z):
    f32, bf16 = jnp.float32, jnp.bfloat16
    field = pltpu.VMEM((24, 16, 1024), f32)
    tiled = pltpu.VMEM((8, 24, 16, 128), f32)
    staged = pltpu.VMEM((8, 16, 24, 128), f32)
    half_y = pltpu.VMEM((2, 8, 192, 128), f32)
    half_z = pltpu.VMEM((3, 128, 1024), f32)
    result = pl.pallas_call(
        kernel,
        out_shape=pltpu.VMEM((8, 24, 16, 128), f32),
        in_specs=[pl.BlockSpec(memory_space=pl.ANY)] * 6,
        out_specs=pl.BlockSpec(memory_space=pltpu.VMEM),
        scratch_shapes=[
            tiled, tiled, pltpu.VMEM((768, 1024), bf16),
            pltpu.VMEM((2, 1024, 1024), bf16), pltpu.VMEM((2, 384, 384), bf16),
            pltpu.VMEM((2, 4, 64, 256), bf16),
            pltpu.VMEM((2, 384, 384), f32), pltpu.VMEM((2, 384, 384), bf16),
            staged, staged, pltpu.VMEM((2, 8, 2, 192, 128), f32), half_y, half_y, staged,
            pltpu.VMEM((3, 4, 64, 1024), f32), half_z, half_z, field,
            pltpu.SemaphoreType.DMA((5,)), pltpu.SemaphoreType.DMA((8,)),
            pltpu.SemaphoreType.DMA((7, CUTS)), pltpu.SemaphoreType.DMA((4, 3)),
        ],
        compiler_params=pltpu.CompilerParams(
            collective_id=0, has_side_effects=True, vmem_limit_bytes=60 * 2**20
        ),
        cost_estimate=pl.CostEstimate(flops=5 * 10**9, bytes_accessed=12 * 2**20, transcendentals=0),
        name="momentum",
    )(u, v, w, deriv_x, deriv_y, deriv_z.reshape(2, 4, 64, 256))
    return jnp.transpose(result, (1, 2, 0, 3)).reshape(24, 16, 1024)


def solution(mesh):
    placed = (P("row", "col", None), P("row", "col", None), P("row", "col", None), P(), P(), P())
    return jax.shard_map(
        shards, mesh=mesh, in_specs=placed, out_specs=P("row", "col", None), check_vma=False
    )
```

```python
import functools

import jax
import jax.numpy as jnp
from jax import lax
from jax.experimental import pallas as pl
from jax.experimental.pallas import tpu as pltpu
from jax.sharding import PartitionSpec as P

viscosity = 0.5
MESH = pl.DeviceIdType.MESH
CUTS = 4
ROWS_OF_CUT = 8 // CUTS
BASE = (0, 288, 336, 144)
SERVED = (144, 48, 48, 144)
ROUTES = ((0, 2), (3, 2), (0, 1), (3, 1), (0, 0), (3, 0), (1, 0), (2, 0))


def split(value):
    high = value.astype(jnp.bfloat16)
    low = (value - high.astype(jnp.float32)).astype(jnp.bfloat16)
    return high, low


def product(matrix, value):
    high, low = split(value)
    return jnp.dot(matrix, high, preferred_element_type=jnp.float32) + jnp.dot(
        matrix, low, preferred_element_type=jnp.float32
    )


def kernel(
    u_hbm, v_hbm, w_hbm, mx_hbm, my_hbm, mz_hbm, total,
    u_own, v_own, u_high, mat_x, mat_y, mat_z, rows_y, lhs_y, u_stage, v_stage,
    u_y, v_y, term_y, back_y, u_z, w_z, term_z, back_z,
    load_sem, send_sem, row_sem, col_sem,
):
    row = lax.axis_index("row")
    col = lax.axis_index("col")
    x_low = (col // 2) % 2
    mine = (col // 4) * 2 + col % 2

    x_me, z_me = row // 8, lax.rem(row, 8)

    def around(z):
        return lax.rem(z + 8, 8)

    def row_of(x, z):
        return x * 8 + around(z)

    def col_peer(shift):
        other = lax.rem(mine + shift, 8)
        return other, (other // 2) * 4 + x_low * 2 + other % 2

    partner = col + 2 - 4 * x_low

    def lanes_of(x):
        return slice(x * 128, (x + 1) * 128)

    for x in range(8):
        pltpu.make_async_copy(u_hbm.at[:, :, lanes_of(x)], u_own.at[x], load_sem.at[0]).start()
    for x in range(8):
        pltpu.make_async_copy(v_hbm.at[:, :, lanes_of(x)], v_own.at[x], load_sem.at[1]).start()

    barrier = pltpu.get_barrier_semaphore()

    def greet(x, z):
        pl.semaphore_signal(barrier, inc=1, device_id=(row_of(x, z), col), device_id_type=MESH)

    for z in (z_me - 2, z_me - 1, z_me + 1, z_me + 2):
        greet(x_me, z)
        greet(1 - x_me, z)
    greet(1 - x_me, z_me)

    @pl.loop(1, 8)
    def _(shift):
        pl.semaphore_signal(
            barrier, inc=1, device_id=(row, col_peer(shift)[1]), device_id_type=MESH
        )

    pl.semaphore_signal(barrier, inc=1, device_id=(row, partner), device_id_type=MESH)
    pltpu.make_async_copy(mx_hbm, mat_x, load_sem.at[2]).start()
    pltpu.make_async_copy(my_hbm, mat_y, load_sem.at[3]).start()
    pltpu.make_async_copy(mz_hbm, mat_z, load_sem.at[4]).start()

    def arrived(ref, sem):
        pltpu.make_async_copy(ref, ref, sem).wait()

    def restage(own, stage, cut):
        flat = own.reshape(8 * 24 * 16, 128)
        for upper in range(2):

            @pl.loop(0, ROWS_OF_CUT)
            def _(step):
                z = upper * 8 + cut * ROWS_OF_CUT + step
                for x in range(8):
                    stage[x, z] = flat[pl.ds(x * 384 + z, 24, stride=16), :]

    def slot(role, j, x):
        served = 2 - j if role == 0 else j
        return pl.ds(pl.multiple_of(BASE[role] + served * 48 + x * 24, 8), 24)

    def over_row(piece, kind, cut, sems):
        for role, j in ROUTES:
            for x in (1 - x_me, x_me):
                src, dst, to = piece(x, j, role)
                if j == 0 and x is x_me:
                    pltpu.make_async_copy(src, dst, sems(role)).start()
                else:
                    pltpu.make_async_remote_copy(
                        src_ref=src, dst_ref=dst, send_sem=send_sem.at[kind],
                        recv_sem=sems(role), device_id=(to, col), device_id_type=MESH,
                    ).start()

    def send_row(stage, pencil, kind, cut):
        rows = pl.ds(cut * ROWS_OF_CUT, ROWS_OF_CUT)

        def piece(x, j, role):
            to = around(z_me + j) if role == 0 else around(z_me - j)
            group = around(to - role)
            src = stage.at[group, pl.ds(x * 8 + cut * ROWS_OF_CUT, ROWS_OF_CUT)]
            if kind == 0:
                dst = pencil.at[role, rows, x_me, pl.ds(pl.multiple_of(z_me * 24, 8), 24), :]
            else:
                dst = pencil.at[rows, slot(role, j, x_me), :]
            return src, dst, x * 8 + to

        over_row(
            piece, kind, cut,
            lambda role: row_sem.at[role, cut] if kind == 0 else row_sem.at[4, cut],
        )

    def pass_on(role, step, cut):
        to = row_of(x_me, z_me + step)
        first = z_me - role - 2 if step == 1 else z_me
        rows = pl.ds(cut * ROWS_OF_CUT, ROWS_OF_CUT)

        @pl.loop(0, 3 + role if step == 1 else 6 - role)
        def _(i):
            z = around(first + i)
            at = pl.ds(pl.multiple_of(z * 24, 8), 24)
            pltpu.make_async_remote_copy(
                src_ref=u_y.at[role, rows, :, at, :],
                dst_ref=u_y.at[role + step, rows, :, at, :],
                send_sem=send_sem.at[7],
                recv_sem=row_sem.at[(5 if step == 1 else 9) + role + step, cut],
                device_id=(to, col), device_id_type=MESH,
            ).start()

    def came_in(role, step, cut):
        count = 2 + role if step == 1 else 5 - role
        arrived(
            v_y.at[pl.ds(cut * ROWS_OF_CUT, ROWS_OF_CUT), pl.ds(0, 48 * count)],
            row_sem.at[(5 if step == 1 else 9) + role, cut],
        )

    def own_part(role, cut):
        arrived(
            v_y.at[pl.ds(cut * ROWS_OF_CUT, ROWS_OF_CUT), pl.ds(BASE[role], SERVED[role])],
            row_sem.at[role, cut],
        )

    def send_col(field, pencil, kind):
        for cut in range(3):

            def piece(to):
                if kind == 0:
                    dst = pencil.at[
                        cut, col // 4, pl.ds(pl.multiple_of((col % 4) * 16, 16), 16), :
                    ]
                else:
                    dst = pencil.at[cut, pl.ds(pl.multiple_of(mine * 16, 16), 16), :]
                return field.at[to * 3 + cut], dst

            @pl.loop(1, 8)
            def _(shift):
                to, to_col = col_peer(shift)
                src, dst = piece(to)
                pltpu.make_async_remote_copy(
                    src_ref=src, dst_ref=dst, send_sem=send_sem.at[3 + kind],
                    recv_sem=col_sem.at[kind, cut], device_id=(row, to_col), device_id_type=MESH,
                ).start()

            src, dst = piece(mine)
            pltpu.make_async_copy(src, dst, col_sem.at[kind, cut]).start()

    arrived(u_own, load_sem.at[0])
    restage(u_own, u_stage, 0)
    pl.semaphore_wait(barrier, 17)
    send_row(u_stage, u_y, 0, 0)
    send_col(u_hbm, u_z, 0)
    for cut in range(1, CUTS):
        restage(u_own, u_stage, cut)
        send_row(u_stage, u_y, 0, cut)
    arrived(v_own, load_sem.at[1])
    for cut in range(CUTS):
        restage(v_own, v_stage, cut)
        send_row(v_stage, v_y, 1, cut)
    send_col(w_hbm, w_z, 1)

    flat_total = total.reshape(8 * 24 * 16, 128)

    for x in range(8):
        high, low = split(u_own[x].reshape(384, 128))
        u_high[:384, lanes_of(x)] = high
        u_high[384:, lanes_of(x)] = low

    arrived(mat_x, load_sem.at[2])

    @pl.loop(0, 4)
    def _(part):
        at = pl.multiple_of(part * 256, 256)

        def along(which):
            both = lax.dot_general(
                u_high[...], mat_x[which, pl.ds(at, 256), :],
                (((1,), (1,)), ((), ())), preferred_element_type=jnp.float32,
            )
            return both[:384] + both[384:]

        first, second = along(0), along(1)
        for i in range(2):
            here = u_own[part * 2 + i].reshape(384, 128)
            term = -here * first[:, lanes_of(i)] + viscosity * second[:, lanes_of(i)]
            total[part * 2 + i] = term.reshape(24, 16, 128)

    arrived(mat_y, load_sem.at[3])
    arrived(mat_z, load_sem.at[4])

    rows_y[...] = mat_y[...].astype(jnp.float32)
    for role in range(4):
        for which in range(2):
            for served in range(SERVED[role] // 48):
                z = around(z_me + (served - 2 if role == 0 else served))
                both_x = [
                    rows_y[which, pl.ds(pl.multiple_of(x * 192 + z * 24, 8), 24), :]
                    for x in range(2)
                ]
                start = 2 * BASE[role] + which * SERVED[role] + served * 48
                lhs_y[start : start + 48, :] = jnp.concatenate(both_x, axis=0).astype(
                    jnp.bfloat16
                )

    half = pl.ds(pl.multiple_of(x_low * 32, 32), 32)
    other_half = pl.ds(pl.multiple_of(32 - x_low * 32, 32), 32)

    def swap(cut):
        region = u_z.at[cut, :, half, :]
        return pltpu.make_async_remote_copy(
            src_ref=region, dst_ref=region, send_sem=send_sem.at[5],
            recv_sem=col_sem.at[3, cut], device_id=(row, partner), device_id_type=MESH,
        )

    def work_y(role, cut):
        base, count = BASE[role], SERVED[role]

        @pl.loop(0, ROWS_OF_CUT // 2)
        def _(pair):
            z = cut * ROWS_OF_CUT + pair * 2
            both = product(
                lhs_y[2 * base : 2 * (base + count), :],
                jnp.concatenate(
                    [u_y[role, z + i].reshape(384, 128) for i in range(2)], axis=1
                ),
            )
            for i in range(2):
                lanes = lanes_of(i)
                term_y[z + i, base : base + count] = (
                    -v_y[z + i, base : base + count] * both[:count, lanes]
                    + viscosity * both[count:, lanes]
                )

    def return_y(cut):
        rows = pl.ds(cut * ROWS_OF_CUT, ROWS_OF_CUT)

        def piece(x, j, role):
            to = around(z_me - j) if role == 0 else around(z_me + j)
            return (
                term_y.at[rows, slot(role, j, x), :],
                back_y.at[
                    around(z_me - role), pl.ds(x_me * 8 + cut * ROWS_OF_CUT, ROWS_OF_CUT)
                ],
                x * 8 + to,
            )

        over_row(piece, 2, cut, lambda role: row_sem.at[5, cut])

    def work_z(cut):
        arrived(u_z.at[cut, :, other_half, :], col_sem.at[3, cut])
        arrived(w_z.at[cut], col_sem.at[1, cut])
        matrix = mat_z[:, :, half, :].reshape(256, 256)
        for tile in range(4):
            lanes = slice(tile * 256, (tile + 1) * 256)
            both = product(matrix, u_z[cut, :, :, lanes].reshape(256, 256))
            term_z[cut, :, lanes] = (
                -w_z[cut, :, lanes] * both[:128] + viscosity * both[128:]
            )

        def piece(to):
            return (
                term_z.at[cut, pl.ds(pl.multiple_of(to * 16, 16), 16), :],
                back_z.at[mine * 3 + cut],
            )

        @pl.loop(1, 8)
        def _(shift):
            to, to_col = col_peer(shift)
            src, dst = piece(to)
            pltpu.make_async_remote_copy(
                src_ref=src, dst_ref=dst, send_sem=send_sem.at[6],
                recv_sem=col_sem.at[2, cut], device_id=(row, to_col), device_id_type=MESH,
            ).start()

        src, dst = piece(mine)
        pltpu.make_async_copy(src, dst, col_sem.at[2, cut]).start()

    for cut in range(CUTS):
        own_part(0, cut)
        pass_on(0, 1, cut)
        own_part(3, cut)
        pass_on(3, -1, cut)
    for cut in range(3):
        arrived(u_z.at[cut, :, half, :], col_sem.at[0, cut])
        swap(cut).start()
    for cut in range(CUTS):
        came_in(1, 1, cut)
        own_part(1, cut)
        pass_on(1, 1, cut)
        came_in(2, -1, cut)
        own_part(2, cut)
        pass_on(2, -1, cut)
    for cut in range(CUTS):
        came_in(2, 1, cut)
        pass_on(2, 1, cut)
        came_in(1, -1, cut)
        pass_on(1, -1, cut)
    for cut in range(max(3, CUTS)):
        if cut < 3:
            work_z(cut)
        if cut < CUTS:
            arrived(v_y.at[pl.ds(cut * ROWS_OF_CUT, ROWS_OF_CUT)], row_sem.at[4, cut])
            came_in(3, 1, cut)
            work_y(3, cut)
            came_in(0, -1, cut)
            work_y(0, cut)
            work_y(1, cut)
            work_y(2, cut)
            return_y(cut)

    for cut in range(3):
        arrived(back_z.at[pl.ds(cut * 8, 8)], col_sem.at[2, cut])

    @pl.loop(0, 24)
    def _(y):
        for x in range(8):
            total[x, y] += back_z[y, :, lanes_of(x)]

    for cut in range(CUTS):
        arrived(back_y.at[:, pl.ds(cut * 2 * ROWS_OF_CUT, 2 * ROWS_OF_CUT)], row_sem.at[5, cut])
        for upper in range(2):

            @pl.loop(0, ROWS_OF_CUT)
            def _(step):
                z = upper * 8 + cut * ROWS_OF_CUT + step
                for x in range(8):
                    flat_total[pl.ds(x * 384 + z, 24, stride=16), :] += back_y[x, z]

    arrived(u_stage.at[:, pl.ds(0, 12)], send_sem.at[0])
    arrived(v_stage.at[:, pl.ds(0, 12)], send_sem.at[1])
    arrived(back_y.at[:, pl.ds(0, 12)], send_sem.at[2])
    arrived(u_y.at[pl.ds(0, 3)], send_sem.at[7])
    arrived(back_z.at[pl.ds(0, 21)], send_sem.at[3])
    arrived(back_z.at[pl.ds(0, 21)], send_sem.at[4])
    arrived(back_z, send_sem.at[5])
    arrived(back_z.at[pl.ds(0, 21)], send_sem.at[6])


def shards(u, v, w, deriv_x, deriv_y, deriv_z):
    f32, bf16 = jnp.float32, jnp.bfloat16
    field = pltpu.VMEM((24, 16, 1024), f32)
    tiled = pltpu.VMEM((8, 24, 16, 128), f32)
    staged = pltpu.VMEM((8, 16, 24, 128), f32)
    served_y = pltpu.VMEM((8, 384, 128), f32)
    half_z = pltpu.VMEM((3, 128, 1024), f32)
    result = pl.pallas_call(
        kernel,
        out_shape=pltpu.VMEM((8, 24, 16, 128), f32),
        in_specs=[pl.BlockSpec(memory_space=pl.ANY)] * 6,
        out_specs=pl.BlockSpec(memory_space=pltpu.VMEM),
        scratch_shapes=[
            tiled, tiled, pltpu.VMEM((768, 1024), bf16),
            pltpu.VMEM((2, 1024, 1024), bf16), pltpu.VMEM((2, 384, 384), bf16),
            pltpu.VMEM((2, 4, 64, 256), bf16),
            pltpu.VMEM((2, 384, 384), f32), pltpu.VMEM((768, 384), bf16),
            staged, staged, pltpu.VMEM((4, 8, 2, 192, 128), f32), served_y, served_y, staged,
            pltpu.VMEM((3, 4, 64, 1024), f32), half_z, half_z, field,
            pltpu.SemaphoreType.DMA((5,)), pltpu.SemaphoreType.DMA((8,)),
            pltpu.SemaphoreType.DMA((12, CUTS)), pltpu.SemaphoreType.DMA((4, 3)),
        ],
        compiler_params=pltpu.CompilerParams(
            collective_id=0, has_side_effects=True, vmem_limit_bytes=60 * 2**20
        ),
        cost_estimate=pl.CostEstimate(flops=5 * 10**9, bytes_accessed=12 * 2**20, transcendentals=0),
        name="momentum",
    )(u, v, w, deriv_x, deriv_y, deriv_z.reshape(2, 4, 64, 256))
    return jnp.transpose(result, (1, 2, 0, 3)).reshape(24, 16, 1024)


def solution(mesh):
    placed = (P("row", "col", None), P("row", "col", None), P("row", "col", None), P(), P(), P())
    return jax.shard_map(
        shards, mesh=mesh, in_specs=placed, out_specs=P("row", "col", None), check_vma=False
    )
```

```python
import functools

import jax
import jax.numpy as jnp
from jax import lax
from jax.experimental import pallas as pl
from jax.experimental.pallas import tpu as pltpu
from jax.sharding import PartitionSpec as P

viscosity = 0.5
MESH = pl.DeviceIdType.MESH
CUT_ROWS = (2, 2, 2, 2)
CUT_AT = (0, 2, 4, 6)
CUTS = len(CUT_ROWS)
BASE = (0, 288, 336, 144)
SERVED = (144, 48, 48, 144)
ROUTES = ((0, 2), (3, 2), (0, 1), (3, 1), (0, 0), (3, 0), (1, 0), (2, 0))


def split(value):
    high = value.astype(jnp.bfloat16)
    low = (value - high.astype(jnp.float32)).astype(jnp.bfloat16)
    return high, low


def product(matrix, value):
    high, low = split(value)
    return jnp.dot(matrix, high, preferred_element_type=jnp.float32) + jnp.dot(
        matrix, low, preferred_element_type=jnp.float32
    )


def kernel(
    u_hbm, v_hbm, w_hbm, mx_hbm, my_hbm, mz_hbm, total,
    u_own, v_own, u_high, mat_x, mat_y, mat_z, rows_y, lhs_y, u_stage, v_stage,
    u_y, v_y, term_y, back_y, u_z, w_z, term_z, back_z,
    load_sem, send_sem, row_sem, col_sem,
):
    row = lax.axis_index("row")
    col = lax.axis_index("col")
    x_low = (col // 2) % 2
    mine = (col // 4) * 2 + col % 2

    x_me, z_me = row // 8, lax.rem(row, 8)

    def around(z):
        return lax.rem(z + 8, 8)

    def row_of(x, z):
        return x * 8 + around(z)

    def col_peer(shift):
        other = lax.rem(mine + shift, 8)
        return other, (other // 2) * 4 + x_low * 2 + other % 2

    partner = col + 2 - 4 * x_low

    def lanes_of(x):
        return slice(x * 128, (x + 1) * 128)

    barrier = pltpu.get_barrier_semaphore()

    def greet(x, z):
        pl.semaphore_signal(barrier, inc=1, device_id=(row_of(x, z), col), device_id_type=MESH)

    for z in (z_me - 2, z_me - 1, z_me + 1, z_me + 2):
        greet(x_me, z)
        greet(1 - x_me, z)
    greet(1 - x_me, z_me)

    @pl.loop(1, 8)
    def _(shift):
        pl.semaphore_signal(
            barrier, inc=1, device_id=(row, col_peer(shift)[1]), device_id_type=MESH
        )

    pl.semaphore_signal(barrier, inc=1, device_id=(row, partner), device_id_type=MESH)

    for x in range(8):
        pltpu.make_async_copy(u_hbm.at[:, :, lanes_of(x)], u_own.at[x], load_sem.at[0]).start()

    def arrived(ref, sem):
        pltpu.make_async_copy(ref, ref, sem).wait()

    def restage(own, stage, cut):
        flat = own.reshape(8 * 24 * 16, 128)
        for upper in range(2):

            @pl.loop(0, CUT_ROWS[cut])
            def _(step):
                z = upper * 8 + CUT_AT[cut] + step
                for x in range(8):
                    stage[x, z] = flat[pl.ds(x * 384 + z, 24, stride=16), :]

    def slot(role, j, x):
        served = 2 - j if role == 0 else j
        return pl.ds(pl.multiple_of(BASE[role] + served * 48 + x * 24, 8), 24)

    def over_row(piece, kind, cut, sems, roles=(0, 1, 2, 3)):
        for x in (1 - x_me, x_me):
            for role, j in ROUTES:
                if role not in roles:
                    continue
                src, dst, to = piece(x, j, role)
                if j == 0 and x is x_me:
                    pltpu.make_async_copy(src, dst, sems(role)).start()
                else:
                    pltpu.make_async_remote_copy(
                        src_ref=src, dst_ref=dst, send_sem=send_sem.at[kind],
                        recv_sem=sems(role), device_id=(to, col), device_id_type=MESH,
                    ).start()

    def send_row(stage, pencil, kind, cut):
        rows = pl.ds(CUT_AT[cut], CUT_ROWS[cut])

        def piece(x, j, role):
            to = around(z_me + j) if role == 0 else around(z_me - j)
            group = around(to - role)
            src = stage.at[group, pl.ds(x * 8 + CUT_AT[cut], CUT_ROWS[cut])]
            if kind == 0:
                dst = pencil.at[role, rows, x_me, pl.ds(pl.multiple_of(z_me * 24, 8), 24), :]
            else:
                dst = pencil.at[rows, slot(role, j, x_me), :]
            return src, dst, x * 8 + to

        over_row(
            piece, kind, cut,
            lambda role: row_sem.at[role, cut] if kind == 0 else row_sem.at[4, cut],
        )

    def pass_on(role, step, cut):
        to = row_of(x_me, z_me + step)
        first = z_me - role - 2 if step == 1 else z_me
        rows = pl.ds(CUT_AT[cut], CUT_ROWS[cut])

        @pl.loop(0, 3 + role if step == 1 else 6 - role)
        def _(i):
            z = around(first + i)
            at = pl.ds(pl.multiple_of(z * 24, 8), 24)
            pltpu.make_async_remote_copy(
                src_ref=u_y.at[role, rows, :, at, :],
                dst_ref=u_y.at[role + step, rows, :, at, :],
                send_sem=send_sem.at[7],
                recv_sem=row_sem.at[(5 if step == 1 else 9) + role + step, cut],
                device_id=(to, col), device_id_type=MESH,
            ).start()

    def came_in(role, step, cut):
        count = 2 + role if step == 1 else 5 - role
        arrived(
            v_y.at[pl.ds(CUT_AT[cut], CUT_ROWS[cut]), pl.ds(0, 48 * count)],
            row_sem.at[(5 if step == 1 else 9) + role, cut],
        )

    def own_part(role, cut):
        arrived(
            v_y.at[pl.ds(CUT_AT[cut], CUT_ROWS[cut]), pl.ds(BASE[role], SERVED[role])],
            row_sem.at[role, cut],
        )

    def send_col(field, pencil, kind):
        for cut in range(3):

            def piece(to):
                if kind == 0:
                    dst = pencil.at[
                        cut, col // 4, pl.ds(pl.multiple_of((col % 4) * 16, 16), 16), :
                    ]
                else:
                    dst = pencil.at[cut, pl.ds(pl.multiple_of(mine * 16, 16), 16), :]
                return field.at[to * 3 + cut], dst

            @pl.loop(1, 8)
            def _(shift):
                to, to_col = col_peer(shift)
                src, dst = piece(to)
                pltpu.make_async_remote_copy(
                    src_ref=src, dst_ref=dst, send_sem=send_sem.at[3 + kind],
                    recv_sem=col_sem.at[kind, cut], device_id=(row, to_col), device_id_type=MESH,
                ).start()

            src, dst = piece(mine)
            pltpu.make_async_copy(src, dst, col_sem.at[kind, cut]).start()

    arrived(u_own, load_sem.at[0])
    for x in range(8):
        pltpu.make_async_copy(v_hbm.at[:, :, lanes_of(x)], v_own.at[x], load_sem.at[1]).start()
    restage(u_own, u_stage, 0)
    pl.semaphore_wait(barrier, 17)
    send_row(u_stage, u_y, 0, 0)
    send_col(u_hbm, u_z, 0)
    for cut in range(1, CUTS):
        restage(u_own, u_stage, cut)
        send_row(u_stage, u_y, 0, cut)
    pltpu.make_async_copy(mx_hbm, mat_x, load_sem.at[2]).start()
    pltpu.make_async_copy(my_hbm, mat_y, load_sem.at[3]).start()
    pltpu.make_async_copy(mz_hbm, mat_z, load_sem.at[4]).start()
    arrived(v_own, load_sem.at[1])
    for cut in range(CUTS):
        restage(v_own, v_stage, cut)
        send_row(v_stage, v_y, 1, cut)
    send_col(w_hbm, w_z, 1)

    flat_total = total.reshape(8 * 24 * 16, 128)

    for x in range(8):
        high, low = split(u_own[x].reshape(384, 128))
        u_high[:384, lanes_of(x)] = high
        u_high[384:, lanes_of(x)] = low

    arrived(mat_x, load_sem.at[2])

    @pl.loop(0, 4)
    def _(part):
        at = pl.multiple_of(part * 256, 256)

        def along(which):
            both = lax.dot_general(
                u_high[...], mat_x[which, pl.ds(at, 256), :],
                (((1,), (1,)), ((), ())), preferred_element_type=jnp.float32,
            )
            return both[:384] + both[384:]

        first, second = along(0), along(1)
        for i in range(2):
            here = u_own[part * 2 + i].reshape(384, 128)
            term = -here * first[:, lanes_of(i)] + viscosity * second[:, lanes_of(i)]
            total[part * 2 + i] = term.reshape(24, 16, 128)

    arrived(mat_y, load_sem.at[3])
    arrived(mat_z, load_sem.at[4])

    rows_y[...] = mat_y[...].astype(jnp.float32)
    for role in range(4):
        for which in range(2):
            for served in range(SERVED[role] // 48):
                z = around(z_me + (served - 2 if role == 0 else served))
                both_x = [
                    rows_y[which, pl.ds(pl.multiple_of(x * 192 + z * 24, 8), 24), :]
                    for x in range(2)
                ]
                start = 2 * BASE[role] + which * SERVED[role] + served * 48
                lhs_y[start : start + 48, :] = jnp.concatenate(both_x, axis=0).astype(
                    jnp.bfloat16
                )

    half = pl.ds(pl.multiple_of(x_low * 32, 32), 32)
    other_half = pl.ds(pl.multiple_of(32 - x_low * 32, 32), 32)

    def swap(cut):
        region = u_z.at[cut, :, half, :]
        return pltpu.make_async_remote_copy(
            src_ref=region, dst_ref=region, send_sem=send_sem.at[5],
            recv_sem=col_sem.at[3, cut], device_id=(row, partner), device_id_type=MESH,
        )

    def work_y(role, cut):
        base, count = BASE[role], SERVED[role]

        at, wide = CUT_AT[cut], CUT_ROWS[cut]
        both = product(
            lhs_y[2 * base : 2 * (base + count), :],
            jnp.concatenate(
                [u_y[role, at + i].reshape(384, 128) for i in range(wide)], axis=1
            ),
        )
        for i in range(wide):
            lanes = lanes_of(i)
            term_y[at + i, base : base + count] = (
                -v_y[at + i, base : base + count] * both[:count, lanes]
                + viscosity * both[count:, lanes]
            )

    def return_y(cut, roles):
        rows = pl.ds(CUT_AT[cut], CUT_ROWS[cut])

        def piece(x, j, role):
            to = around(z_me - j) if role == 0 else around(z_me + j)
            return (
                term_y.at[rows, slot(role, j, x), :],
                back_y.at[
                    around(z_me - role), pl.ds(x_me * 8 + CUT_AT[cut], CUT_ROWS[cut])
                ],
                x * 8 + to,
            )

        over_row(piece, 2, cut, lambda role: row_sem.at[5, cut], roles)

    def work_z(cut):
        arrived(u_z.at[cut, :, other_half, :], col_sem.at[3, cut])
        arrived(w_z.at[cut], col_sem.at[1, cut])
        matrix = mat_z[:, :, half, :].reshape(256, 256)
        for tile in range(4):
            lanes = slice(tile * 256, (tile + 1) * 256)
            both = product(matrix, u_z[cut, :, :, lanes].reshape(256, 256))
            term_z[cut, :, lanes] = (
                -w_z[cut, :, lanes] * both[:128] + viscosity * both[128:]
            )

        def piece(to):
            return (
                term_z.at[cut, pl.ds(pl.multiple_of(to * 16, 16), 16), :],
                back_z.at[mine * 3 + cut],
            )

        @pl.loop(1, 8)
        def _(shift):
            to, to_col = col_peer(shift)
            src, dst = piece(to)
            pltpu.make_async_remote_copy(
                src_ref=src, dst_ref=dst, send_sem=send_sem.at[6],
                recv_sem=col_sem.at[2, cut], device_id=(row, to_col), device_id_type=MESH,
            ).start()

        src, dst = piece(mine)
        pltpu.make_async_copy(src, dst, col_sem.at[2, cut]).start()

    for cut in range(CUTS):
        own_part(0, cut)
        pass_on(0, 1, cut)
        own_part(3, cut)
        pass_on(3, -1, cut)
    for cut in range(3):
        arrived(u_z.at[cut, :, half, :], col_sem.at[0, cut])
        swap(cut).start()
    for cut in range(CUTS):
        came_in(1, 1, cut)
        own_part(1, cut)
        pass_on(1, 1, cut)
        came_in(2, -1, cut)
        own_part(2, cut)
        pass_on(2, -1, cut)
    for cut in range(CUTS):
        came_in(2, 1, cut)
        pass_on(2, 1, cut)
        came_in(1, -1, cut)
        pass_on(1, -1, cut)
    for cut in range(max(3, CUTS)):
        if cut < 3:
            work_z(cut)
        if cut < CUTS:
            arrived(v_y.at[pl.ds(CUT_AT[cut], CUT_ROWS[cut])], row_sem.at[4, cut])
            work_y(1, cut)
            work_y(2, cut)
            return_y(cut, (1, 2))
            came_in(3, 1, cut)
            work_y(3, cut)
            return_y(cut, (3,))
            came_in(0, -1, cut)
            work_y(0, cut)
            return_y(cut, (0,))

    for cut in range(3):
        arrived(back_z.at[pl.ds(cut * 8, 8)], col_sem.at[2, cut])

    @pl.loop(0, 24)
    def _(y):
        for x in range(8):
            total[x, y] += back_z[y, :, lanes_of(x)]

    for cut in range(CUTS):
        arrived(back_y.at[:, pl.ds(0, 2 * CUT_ROWS[cut])], row_sem.at[5, cut])
        for upper in range(2):

            @pl.loop(0, CUT_ROWS[cut])
            def _(step):
                z = upper * 8 + CUT_AT[cut] + step
                for x in range(8):
                    flat_total[pl.ds(x * 384 + z, 24, stride=16), :] += back_y[x, z]

    arrived(u_stage.at[:, pl.ds(0, 12)], send_sem.at[0])
    arrived(v_stage.at[:, pl.ds(0, 12)], send_sem.at[1])
    arrived(back_y.at[:, pl.ds(0, 12)], send_sem.at[2])
    arrived(u_y.at[pl.ds(0, 3)], send_sem.at[7])
    arrived(back_z.at[pl.ds(0, 21)], send_sem.at[3])
    arrived(back_z.at[pl.ds(0, 21)], send_sem.at[4])
    arrived(back_z, send_sem.at[5])
    arrived(back_z.at[pl.ds(0, 21)], send_sem.at[6])


def shards(u, v, w, deriv_x, deriv_y, deriv_z):
    f32, bf16 = jnp.float32, jnp.bfloat16
    field = pltpu.VMEM((24, 16, 1024), f32)
    tiled = pltpu.VMEM((8, 24, 16, 128), f32)
    staged = pltpu.VMEM((8, 16, 24, 128), f32)
    served_y = pltpu.VMEM((8, 384, 128), f32)
    half_z = pltpu.VMEM((3, 128, 1024), f32)
    result = pl.pallas_call(
        kernel,
        out_shape=pltpu.VMEM((8, 24, 16, 128), f32),
        in_specs=[pl.BlockSpec(memory_space=pl.ANY)] * 6,
        out_specs=pl.BlockSpec(memory_space=pltpu.VMEM),
        scratch_shapes=[
            tiled, tiled, pltpu.VMEM((768, 1024), bf16),
            pltpu.VMEM((2, 1024, 1024), bf16), pltpu.VMEM((2, 384, 384), bf16),
            pltpu.VMEM((2, 4, 64, 256), bf16),
            pltpu.VMEM((2, 384, 384), f32), pltpu.VMEM((768, 384), bf16),
            staged, staged, pltpu.VMEM((4, 8, 2, 192, 128), f32), served_y, served_y, staged,
            pltpu.VMEM((3, 4, 64, 1024), f32), half_z, half_z, field,
            pltpu.SemaphoreType.DMA((5,)), pltpu.SemaphoreType.DMA((8,)),
            pltpu.SemaphoreType.DMA((12, CUTS)), pltpu.SemaphoreType.DMA((4, 3)),
        ],
        compiler_params=pltpu.CompilerParams(
            collective_id=0, has_side_effects=True, vmem_limit_bytes=60 * 2**20
        ),
        cost_estimate=pl.CostEstimate(flops=5 * 10**9, bytes_accessed=12 * 2**20, transcendentals=0),
        name="momentum",
    )(u, v, w, deriv_x, deriv_y, deriv_z.reshape(2, 4, 64, 256))
    return jnp.transpose(result, (1, 2, 0, 3)).reshape(24, 16, 1024)


def solution(mesh):
    placed = (P("row", "col", None), P("row", "col", None), P("row", "col", None), P(), P(), P())
    return jax.shard_map(
        shards, mesh=mesh, in_specs=placed, out_specs=P("row", "col", None), check_vma=False
    )
```

```python
import functools

import jax
import jax.numpy as jnp
from jax import lax
from jax.experimental import pallas as pl
from jax.experimental.pallas import tpu as pltpu
from jax.sharding import PartitionSpec as P

viscosity = 0.5
MESH = pl.DeviceIdType.MESH
CUT_ROWS = (2, 2, 2, 2)
CUT_AT = (0, 2, 4, 6)
CUTS = len(CUT_ROWS)
BASE = (0, 288, 336, 144)
SERVED = (144, 48, 48, 144)
ROUTES = ((0, 2), (3, 2), (0, 1), (3, 1), (0, 0), (3, 0), (1, 0), (2, 0))


def split(value):
    high = value.astype(jnp.bfloat16)
    low = (value - high.astype(jnp.float32)).astype(jnp.bfloat16)
    return high, low


def product(matrix, value):
    high, low = split(value)
    return jnp.dot(matrix, high, preferred_element_type=jnp.float32) + jnp.dot(
        matrix, low, preferred_element_type=jnp.float32
    )


def kernel(
    u_hbm, v_hbm, w_hbm, mx_hbm, my_hbm, mz_hbm, total,
    u_own, v_own, u_high, mat_x, mat_y, mat_z, rows_y, lhs_y, u_stage, v_stage,
    u_y, v_y, term_y, back_y, u_z, w_z, term_z, back_z,
    load_sem, send_sem, row_sem, col_sem,
):
    row = lax.axis_index("row")
    col = lax.axis_index("col")
    x_low = (col // 2) % 2
    mine = (col // 4) * 2 + col % 2

    x_me, z_me = row // 8, lax.rem(row, 8)

    def around(z):
        return lax.rem(z + 8, 8)

    def row_of(x, z):
        return x * 8 + around(z)

    def col_peer(shift):
        other = lax.rem(mine + shift, 8)
        return other, (other // 2) * 4 + x_low * 2 + other % 2

    partner = col + 2 - 4 * x_low

    def lanes_of(x):
        return slice(x * 128, (x + 1) * 128)

    barrier = pltpu.get_barrier_semaphore()

    def greet(x, z):
        pl.semaphore_signal(barrier, inc=1, device_id=(row_of(x, z), col), device_id_type=MESH)

    for z in (z_me - 2, z_me - 1, z_me + 1, z_me + 2):
        greet(x_me, z)
        greet(1 - x_me, z)
    greet(1 - x_me, z_me)

    @pl.loop(1, 8)
    def _(shift):
        pl.semaphore_signal(
            barrier, inc=1, device_id=(row, col_peer(shift)[1]), device_id_type=MESH
        )

    pl.semaphore_signal(barrier, inc=1, device_id=(row, partner), device_id_type=MESH)

    for x in range(8):
        pltpu.make_async_copy(u_hbm.at[:, :, lanes_of(x)], u_own.at[x], load_sem.at[0]).start()

    def arrived(ref, sem):
        pltpu.make_async_copy(ref, ref, sem).wait()

    def restage(own, stage, cut):
        flat = own.reshape(8 * 24 * 16, 128)
        for upper in range(2):

            @pl.loop(0, CUT_ROWS[cut])
            def _(step):
                z = upper * 8 + CUT_AT[cut] + step
                for x in range(8):
                    stage[x, z] = flat[pl.ds(x * 384 + z, 24, stride=16), :]

    def slot(role, j, x):
        served = 2 - j if role == 0 else j
        return pl.ds(pl.multiple_of(BASE[role] + served * 48 + x * 24, 8), 24)

    def over_row(piece, kind, cut, sems, roles=(0, 1, 2, 3), sides=(1, 0)):
        for side in sides:
            x = 1 - x_me if side else x_me
            for role, j in ROUTES:
                if role not in roles:
                    continue
                src, dst, to = piece(x, j, role)
                if j == 0 and not side:
                    pltpu.make_async_copy(src, dst, sems(role)).start()
                else:
                    pltpu.make_async_remote_copy(
                        src_ref=src, dst_ref=dst, send_sem=send_sem.at[kind],
                        recv_sem=sems(role), device_id=(to, col), device_id_type=MESH,
                    ).start()

    def send_row(stage, pencil, kind, cut, sides=(1, 0)):
        rows = pl.ds(CUT_AT[cut], CUT_ROWS[cut])

        def piece(x, j, role):
            to = around(z_me + j) if role == 0 else around(z_me - j)
            group = around(to - role)
            src = stage.at[group, pl.ds(x * 8 + CUT_AT[cut], CUT_ROWS[cut])]
            if kind == 0:
                dst = pencil.at[role, rows, x_me, pl.ds(pl.multiple_of(z_me * 24, 8), 24), :]
            else:
                dst = pencil.at[rows, slot(role, j, x_me), :]
            return src, dst, x * 8 + to

        over_row(
            piece, kind, cut,
            lambda role: row_sem.at[role, cut] if kind == 0 else row_sem.at[4, cut],
            sides=sides,
        )

    def pass_on(role, step, cut):
        to = row_of(x_me, z_me + step)
        first = z_me - role - 2 if step == 1 else z_me
        rows = pl.ds(CUT_AT[cut], CUT_ROWS[cut])

        @pl.loop(0, 3 + role if step == 1 else 6 - role)
        def _(i):
            z = around(first + i)
            at = pl.ds(pl.multiple_of(z * 24, 8), 24)
            pltpu.make_async_remote_copy(
                src_ref=u_y.at[role, rows, :, at, :],
                dst_ref=u_y.at[role + step, rows, :, at, :],
                send_sem=send_sem.at[7],
                recv_sem=row_sem.at[(5 if step == 1 else 9) + role + step, cut],
                device_id=(to, col), device_id_type=MESH,
            ).start()

    def came_in(role, step, cut):
        count = 2 + role if step == 1 else 5 - role
        arrived(
            v_y.at[pl.ds(CUT_AT[cut], CUT_ROWS[cut]), pl.ds(0, 48 * count)],
            row_sem.at[(5 if step == 1 else 9) + role, cut],
        )

    def own_part(role, cut):
        arrived(
            v_y.at[pl.ds(CUT_AT[cut], CUT_ROWS[cut]), pl.ds(BASE[role], SERVED[role])],
            row_sem.at[role, cut],
        )

    def send_col(field, pencil, kind):
        for cut in range(3):

            def piece(to):
                if kind == 0:
                    dst = pencil.at[
                        cut, col // 4, pl.ds(pl.multiple_of((col % 4) * 16, 16), 16), :
                    ]
                else:
                    dst = pencil.at[cut, pl.ds(pl.multiple_of(mine * 16, 16), 16), :]
                return field.at[to * 3 + cut], dst

            @pl.loop(1, 8)
            def _(shift):
                to, to_col = col_peer(shift)
                src, dst = piece(to)
                pltpu.make_async_remote_copy(
                    src_ref=src, dst_ref=dst, send_sem=send_sem.at[3 + kind],
                    recv_sem=col_sem.at[kind, cut], device_id=(row, to_col), device_id_type=MESH,
                ).start()

            src, dst = piece(mine)
            pltpu.make_async_copy(src, dst, col_sem.at[kind, cut]).start()

    arrived(u_own, load_sem.at[0])
    for x in range(8):
        pltpu.make_async_copy(v_hbm.at[:, :, lanes_of(x)], v_own.at[x], load_sem.at[1]).start()
    restage(u_own, u_stage, 0)
    pl.semaphore_wait(barrier, 17)
    send_row(u_stage, u_y, 0, 0)
    send_col(u_hbm, u_z, 0)
    for cut in range(1, CUTS):
        restage(u_own, u_stage, cut)
        send_row(u_stage, u_y, 0, cut)
    pltpu.make_async_copy(mx_hbm, mat_x, load_sem.at[2]).start()
    pltpu.make_async_copy(my_hbm, mat_y, load_sem.at[3]).start()
    pltpu.make_async_copy(mz_hbm, mat_z, load_sem.at[4]).start()
    arrived(v_own, load_sem.at[1])
    for cut in range(CUTS):
        restage(v_own, v_stage, cut)
        send_row(v_stage, v_y, 1, cut, (1,))
    for cut in range(CUTS):
        send_row(v_stage, v_y, 1, cut, (0,))
    send_col(w_hbm, w_z, 1)

    flat_total = total.reshape(8 * 24 * 16, 128)

    for x in range(8):
        high, low = split(u_own[x].reshape(384, 128))
        u_high[:384, lanes_of(x)] = high
        u_high[384:, lanes_of(x)] = low

    arrived(mat_x, load_sem.at[2])

    @pl.loop(0, 4)
    def _(part):
        at = pl.multiple_of(part * 256, 256)

        def along(which):
            both = lax.dot_general(
                u_high[...], mat_x[which, pl.ds(at, 256), :],
                (((1,), (1,)), ((), ())), preferred_element_type=jnp.float32,
            )
            return both[:384] + both[384:]

        first, second = along(0), along(1)
        for i in range(2):
            here = u_own[part * 2 + i].reshape(384, 128)
            term = -here * first[:, lanes_of(i)] + viscosity * second[:, lanes_of(i)]
            total[part * 2 + i] = term.reshape(24, 16, 128)

    arrived(mat_y, load_sem.at[3])
    arrived(mat_z, load_sem.at[4])

    rows_y[...] = mat_y[...].astype(jnp.float32)
    for role in range(4):
        for which in range(2):
            for served in range(SERVED[role] // 48):
                z = around(z_me + (served - 2 if role == 0 else served))
                both_x = [
                    rows_y[which, pl.ds(pl.multiple_of(x * 192 + z * 24, 8), 24), :]
                    for x in range(2)
                ]
                start = 2 * BASE[role] + which * SERVED[role] + served * 48
                lhs_y[start : start + 48, :] = jnp.concatenate(both_x, axis=0).astype(
                    jnp.bfloat16
                )

    half = pl.ds(pl.multiple_of(x_low * 32, 32), 32)
    other_half = pl.ds(pl.multiple_of(32 - x_low * 32, 32), 32)

    def swap(cut):
        region = u_z.at[cut, :, half, :]
        return pltpu.make_async_remote_copy(
            src_ref=region, dst_ref=region, send_sem=send_sem.at[5],
            recv_sem=col_sem.at[3, cut], device_id=(row, partner), device_id_type=MESH,
        )

    def work_y(role, cut):
        base, count = BASE[role], SERVED[role]

        at, wide = CUT_AT[cut], CUT_ROWS[cut]
        both = product(
            lhs_y[2 * base : 2 * (base + count), :],
            jnp.concatenate(
                [u_y[role, at + i].reshape(384, 128) for i in range(wide)], axis=1
            ),
        )
        for i in range(wide):
            lanes = lanes_of(i)
            term_y[at + i, base : base + count] = (
                -v_y[at + i, base : base + count] * both[:count, lanes]
                + viscosity * both[count:, lanes]
            )

    def return_y(cut, roles):
        rows = pl.ds(CUT_AT[cut], CUT_ROWS[cut])

        def piece(x, j, role):
            to = around(z_me - j) if role == 0 else around(z_me + j)
            return (
                term_y.at[rows, slot(role, j, x), :],
                back_y.at[
                    around(z_me - role), pl.ds(x_me * 8 + CUT_AT[cut], CUT_ROWS[cut])
                ],
                x * 8 + to,
            )

        over_row(piece, 2, cut, lambda role: row_sem.at[5, cut], roles)

    def work_z(cut):
        arrived(u_z.at[cut, :, other_half, :], col_sem.at[3, cut])
        arrived(w_z.at[cut], col_sem.at[1, cut])
        matrix = mat_z[:, :, half, :].reshape(256, 256)
        for tile in range(4):
            lanes = slice(tile * 256, (tile + 1) * 256)
            both = product(matrix, u_z[cut, :, :, lanes].reshape(256, 256))
            term_z[cut, :, lanes] = (
                -w_z[cut, :, lanes] * both[:128] + viscosity * both[128:]
            )

        def piece(to):
            return (
                term_z.at[cut, pl.ds(pl.multiple_of(to * 16, 16), 16), :],
                back_z.at[mine * 3 + cut],
            )

        @pl.loop(1, 8)
        def _(shift):
            to, to_col = col_peer(shift)
            src, dst = piece(to)
            pltpu.make_async_remote_copy(
                src_ref=src, dst_ref=dst, send_sem=send_sem.at[6],
                recv_sem=col_sem.at[2, cut], device_id=(row, to_col), device_id_type=MESH,
            ).start()

        src, dst = piece(mine)
        pltpu.make_async_copy(src, dst, col_sem.at[2, cut]).start()

    for cut in range(CUTS):
        own_part(0, cut)
        pass_on(0, 1, cut)
        own_part(3, cut)
        pass_on(3, -1, cut)
    for cut in range(3):
        arrived(u_z.at[cut, :, half, :], col_sem.at[0, cut])
        swap(cut).start()
    for cut in range(CUTS):
        came_in(1, 1, cut)
        own_part(1, cut)
        pass_on(1, 1, cut)
        came_in(2, -1, cut)
        own_part(2, cut)
        pass_on(2, -1, cut)
    for cut in range(CUTS):
        came_in(2, 1, cut)
        pass_on(2, 1, cut)
        came_in(1, -1, cut)
        pass_on(1, -1, cut)
    for cut in range(max(3, CUTS)):
        if cut < 3:
            work_z(cut)
        if cut < CUTS:
            arrived(v_y.at[pl.ds(CUT_AT[cut], CUT_ROWS[cut])], row_sem.at[4, cut])
            work_y(1, cut)
            work_y(2, cut)
            return_y(cut, (1, 2))
            came_in(3, 1, cut)
            work_y(3, cut)
            return_y(cut, (3,))
            came_in(0, -1, cut)
            work_y(0, cut)
            return_y(cut, (0,))

    for cut in range(3):
        arrived(back_z.at[pl.ds(cut * 8, 8)], col_sem.at[2, cut])

    @pl.loop(0, 24)
    def _(y):
        for x in range(8):
            total[x, y] += back_z[y, :, lanes_of(x)]

    for cut in range(CUTS):
        arrived(back_y.at[:, pl.ds(0, 2 * CUT_ROWS[cut])], row_sem.at[5, cut])
        for upper in range(2):

            @pl.loop(0, CUT_ROWS[cut])
            def _(step):
                z = upper * 8 + CUT_AT[cut] + step
                for x in range(8):
                    flat_total[pl.ds(x * 384 + z, 24, stride=16), :] += back_y[x, z]

    arrived(u_stage.at[:, pl.ds(0, 12)], send_sem.at[0])
    arrived(v_stage.at[:, pl.ds(0, 12)], send_sem.at[1])
    arrived(back_y.at[:, pl.ds(0, 12)], send_sem.at[2])
    arrived(u_y.at[pl.ds(0, 3)], send_sem.at[7])
    arrived(back_z.at[pl.ds(0, 21)], send_sem.at[3])
    arrived(back_z.at[pl.ds(0, 21)], send_sem.at[4])
    arrived(back_z, send_sem.at[5])
    arrived(back_z.at[pl.ds(0, 21)], send_sem.at[6])


def shards(u, v, w, deriv_x, deriv_y, deriv_z):
    f32, bf16 = jnp.float32, jnp.bfloat16
    field = pltpu.VMEM((24, 16, 1024), f32)
    tiled = pltpu.VMEM((8, 24, 16, 128), f32)
    staged = pltpu.VMEM((8, 16, 24, 128), f32)
    served_y = pltpu.VMEM((8, 384, 128), f32)
    half_z = pltpu.VMEM((3, 128, 1024), f32)
    result = pl.pallas_call(
        kernel,
        out_shape=pltpu.VMEM((8, 24, 16, 128), f32),
        in_specs=[pl.BlockSpec(memory_space=pl.ANY)] * 6,
        out_specs=pl.BlockSpec(memory_space=pltpu.VMEM),
        scratch_shapes=[
            tiled, tiled, pltpu.VMEM((768, 1024), bf16),
            pltpu.VMEM((2, 1024, 1024), bf16), pltpu.VMEM((2, 384, 384), bf16),
            pltpu.VMEM((2, 4, 64, 256), bf16),
            pltpu.VMEM((2, 384, 384), f32), pltpu.VMEM((768, 384), bf16),
            staged, staged, pltpu.VMEM((4, 8, 2, 192, 128), f32), served_y, served_y, staged,
            pltpu.VMEM((3, 4, 64, 1024), f32), half_z, half_z, field,
            pltpu.SemaphoreType.DMA((5,)), pltpu.SemaphoreType.DMA((8,)),
            pltpu.SemaphoreType.DMA((12, CUTS)), pltpu.SemaphoreType.DMA((4, 3)),
        ],
        compiler_params=pltpu.CompilerParams(
            collective_id=0, has_side_effects=True, vmem_limit_bytes=60 * 2**20
        ),
        cost_estimate=pl.CostEstimate(flops=5 * 10**9, bytes_accessed=12 * 2**20, transcendentals=0),
        name="momentum",
    )(u, v, w, deriv_x, deriv_y, deriv_z.reshape(2, 4, 64, 256))
    return jnp.transpose(result, (1, 2, 0, 3)).reshape(24, 16, 1024)


def solution(mesh):
    placed = (P("row", "col", None), P("row", "col", None), P("row", "col", None), P(), P(), P())
    return jax.shard_map(
        shards, mesh=mesh, in_specs=placed, out_specs=P("row", "col", None), check_vma=False
    )
```
